32 devices in a mesh: seq: 16 (over z, x, core), head: 2 (over y).
Axes of the slice: x: 2, y: 2, z: 4, core: 2. Of those that a mesh axis runs over, the one named last changes fastest.
Arguments:
- queries: bfloat16 [8192, 4096], P(('seq', 'head')), may hold values from -8 to 8
- keys: bfloat16 [8192, 2048], P(('seq', 'head')), may hold values from -8 to 8
- values: bfloat16 [8192, 2048], P(('seq', 'head')), may hold values from -6 to 6
- output_cotangent: bfloat16 [8192, 4096], P(('seq', 'head')), may hold values from -6 to 6
Outputs:
- attended: bfloat16 [8192, 4096], P(('seq', 'head'))
- grad_queries: bfloat16 [8192, 4096], P(('seq', 'head'))
- key_gradient: bfloat16 [8192, 2048], P(('seq', 'head'))
- value_gradient: bfloat16 [8192, 2048], P(('seq', 'head'))
The draws below stay inside these ranges and needn't reach their ends.
All inputs are finite; a program needn't handle non-finite values.
Results may differ from the reference program's by a relative error of at most 0.0095.
Values may be sent and summed in bfloat16 or wider, within the bound.
A program may use at most 128 MiB of HBM per device.

```python
import jax
import jax.numpy as jnp
from jax import lax

QUERY_HEADS = 32
KEY_VALUE_HEADS = 16
HEAD_SIZE = 128
WINDOW_TOKENS = 1024
TOK_SEQ = 512
SLAB_TOKENS = 8192


def draw_pair(key):
    base = jax.random.fold_in(key, 11)
    key_q, key_rows_local = jax.random.split(base, 2)
    query_entries = jnp.clip(jax.random.normal(key_q, (SLAB_TOKENS, QUERY_HEADS, HEAD_SIZE), jnp.float32), -6.0, 6.0)
    key_entries = jnp.clip(jax.random.normal(key_rows_local, (SLAB_TOKENS, KEY_VALUE_HEADS, HEAD_SIZE), jnp.float32), -6.0, 6.0)
    query_entries = jnp.clip(query_entries, -8.0, 8.0)
    key_entries = jnp.clip(key_entries, -8.0, 8.0)
    return (query_entries.reshape(SLAB_TOKENS, QUERY_HEADS * HEAD_SIZE), key_entries.reshape(SLAB_TOKENS, KEY_VALUE_HEADS * HEAD_SIZE))


def draw_queries(key, part):
    return draw_pair(key)[0].astype(jnp.bfloat16)


def draw_keys(key, part):
    return draw_pair(key)[1].astype(jnp.bfloat16)


def level_of(own_key, dims, pieces, smallest, largest):
    level, own = 1.0, jax.random.fold_in(own_key, 6)
    for axis_at, shards_of in pieces:
        steps = jnp.exp(jax.random.uniform(jax.random.fold_in(own, axis_at), (shards_of,), jnp.float32, smallest / len(pieces), largest / len(pieces)))
        level = level * jnp.repeat(steps, dims[axis_at] // shards_of).reshape([-1 if axis == axis_at else 1 for axis in range(len(dims))])
    return level


def bell_draw(own_key, shape, deviation, most, cuts=(), kind=jnp.bfloat16):
    entries = jax.random.normal(own_key, shape, jnp.float32) * deviation
    if len(cuts) > 0:
        entries = level_of(own_key, shape, cuts, -0.22, 0.18) * entries
    return jnp.clip(entries, min=-most, max=most).astype(kind)


def setup_inputs(seed: int = 0) -> dict:
    key_list = jax.random.split(jax.random.key(seed), 5)
    return {
        "queries": draw_queries(jax.random.fold_in(key_list[4], 71), 0),
        "keys": draw_keys(jax.random.fold_in(key_list[4], 71), 0),
        "values": bell_draw(key_list[2], (SLAB_TOKENS, KEY_VALUE_HEADS * HEAD_SIZE), 1.0, 6.0, ((0, 32),)),
        "output_cotangent": bell_draw(key_list[3], (SLAB_TOKENS, QUERY_HEADS * HEAD_SIZE), 1.0, 6.0, ((0, 32),)),
    }


query_scale = 168.0 ** -0.5


def mix(form, left, right):
    return jnp.einsum(form, left.astype(jnp.float32), right.astype(jnp.float32))


def head_pass(query_head, key_extended, value_extended, grad_head, start, block):
    group_factor, total_count, width = query_head.shape
    steps = total_count // block
    rows = jnp.arange(block, dtype=jnp.int32)[:, None]
    cols = jnp.arange(WINDOW_TOKENS + block, dtype=jnp.int32)[None, :]

    def visit(carry, index):
        dk_acc, dv_acc = carry
        anchor = index * block
        query_blk = lax.dynamic_slice_in_dim(query_head, anchor, block, 1)
        grad_blk = lax.dynamic_slice_in_dim(grad_head, anchor, block, 1)
        key_slab = lax.dynamic_slice_in_dim(key_extended, anchor, WINDOW_TOKENS + block, 0)
        value_slab = lax.dynamic_slice_in_dim(value_extended, anchor, WINDOW_TOKENS + block, 0)
        key_pos = start + anchor + cols - WINDOW_TOKENS
        allowed = (cols > rows) & (cols <= rows + WINDOW_TOKENS) & (key_pos >= 0)
        scores = query_scale * mix("rqd,kd->rqk", query_blk, key_slab)
        scores = jnp.where(allowed[None], scores, -1e30)
        top = jnp.max(scores, axis=-1, keepdims=True)
        lse = top + jnp.log(jnp.sum(jnp.exp(scores - top), axis=-1, keepdims=True))
        probs = jnp.exp(scores - lse)
        probs_b = probs.astype(jnp.bfloat16)
        out_b = mix("rqk,kd->rqd", probs_b, value_slab).astype(jnp.bfloat16)
        delta = jnp.sum(grad_blk.astype(jnp.float32) * out_b.astype(jnp.float32), axis=-1)
        dprobs = mix("rqd,kd->rqk", grad_blk, value_slab)
        dscores = (probs * (dprobs - delta[..., None])).astype(jnp.bfloat16)
        dq_b = (query_scale * mix("rqk,kd->rqd", dscores, key_slab)).astype(jnp.bfloat16)
        dk_slab = query_scale * mix("rqk,rqd->kd", dscores, query_blk)
        dv_slab = mix("rqk,rqd->kd", probs_b, grad_blk)
        dk_acc = lax.dynamic_update_slice_in_dim(dk_acc, lax.dynamic_slice_in_dim(dk_acc, anchor, WINDOW_TOKENS + block, 0) + dk_slab, anchor, 0)
        dv_acc = lax.dynamic_update_slice_in_dim(dv_acc, lax.dynamic_slice_in_dim(dv_acc, anchor, WINDOW_TOKENS + block, 0) + dv_slab, anchor, 0)
        return (dk_acc, dv_acc), (out_b, dq_b)

    empty = jnp.zeros((WINDOW_TOKENS + total_count, width), jnp.float32)
    (dk_acc, dv_acc), (outs, grads) = lax.scan(visit, (empty, empty), jnp.arange(steps, dtype=jnp.int32))
    outs = outs.transpose(1, 0, 2, 3).reshape(group_factor, total_count, width)
    grads = grads.transpose(1, 0, 2, 3).reshape(group_factor, total_count, width)
    return outs, grads, dk_acc, dv_acc


def reference(queries, keys, values, output_cotangent):
    total_count = queries.shape[0]
    group_factor = QUERY_HEADS // KEY_VALUE_HEADS
    block = min(512, TOK_SEQ)
    query_head_rows = queries.reshape(total_count, KEY_VALUE_HEADS, group_factor, HEAD_SIZE).transpose(1, 2, 0, 3)
    head_gradients = output_cotangent.reshape(total_count, KEY_VALUE_HEADS, group_factor, HEAD_SIZE).transpose(1, 2, 0, 3)
    leading_part = jnp.zeros((WINDOW_TOKENS, KEY_VALUE_HEADS * HEAD_SIZE), keys.dtype)
    key_extended = jnp.concatenate([leading_part, keys], 0).reshape(WINDOW_TOKENS + total_count, KEY_VALUE_HEADS, HEAD_SIZE).transpose(1, 0, 2)
    value_extended = jnp.concatenate([leading_part, values], 0).reshape(WINDOW_TOKENS + total_count, KEY_VALUE_HEADS, HEAD_SIZE).transpose(1, 0, 2)

    def per_head(parts):
        return head_pass(parts[0], parts[1], parts[2], parts[3], 0, block)

    outs, grads_q, key_grad_parts, value_grad_parts = lax.map(per_head, (query_head_rows, key_extended, value_extended, head_gradients))
    attended = outs.transpose(2, 0, 1, 3).reshape(total_count, QUERY_HEADS * HEAD_SIZE)
    grad_queries = grads_q.transpose(2, 0, 1, 3).reshape(total_count, QUERY_HEADS * HEAD_SIZE)
    key_gradient = key_grad_parts[:, WINDOW_TOKENS:].transpose(1, 0, 2).reshape(total_count, KEY_VALUE_HEADS * HEAD_SIZE).astype(jnp.bfloat16)
    value_gradient = value_grad_parts[:, WINDOW_TOKENS:].transpose(1, 0, 2).reshape(total_count, KEY_VALUE_HEADS * HEAD_SIZE).astype(jnp.bfloat16)
    return (attended, grad_queries, key_gradient, value_gradient)
```

```python
import functools

import jax
import jax.numpy as jnp
from jax import lax
from jax.experimental import pallas as pl
from jax.experimental.pallas import tpu as pltpu
from jax.sharding import PartitionSpec as P

HEAD_SIZE = 128
WINDOW_TOKENS = 1024
TILE = 256
MESH = pl.DeviceIdType.MESH

query_scale = 168.0 ** (-0.5)
exponent_scale = query_scale * 1.4426950408889634
HIDDEN = -1e30


def matmul(left, right):
    return jnp.dot(left, right, preferred_element_type=jnp.float32)


def matmul_nt(left, right):
    return lax.dot_general(left, right, (((1,), (1,)), ((), ())), preferred_element_type=jnp.float32)


def turned(value):
    return value.astype(jnp.float32).T


def attend(n, factor, first, qb, gb, kb, vb, kt, vt, ob, dqb, dk, dv):
    width = HEAD_SIZE
    chunks = WINDOW_TOKENS // TILE
    dk[n] = jnp.zeros(dk.shape[1:], jnp.float32)
    dv[n] = jnp.zeros(dv.shape[1:], jnp.float32)

    def turn(at, _):
        row = pl.multiple_of(at * TILE, TILE)
        kt[:, pl.ds(row, TILE)] = turned(kb[n, pl.ds(row, TILE), :]).astype(jnp.bfloat16)
        vt[:, pl.ds(row, TILE)] = turned(vb[n, pl.ds(row, TILE), :]).astype(jnp.bfloat16)
        return 0

    lax.fori_loop(0, kb.shape[1] // TILE, turn, 0)
    key_at = lax.broadcasted_iota(jnp.int32, (TILE, TILE), 0)
    query_at = lax.broadcasted_iota(jnp.int32, (TILE, TILE), 1)

    def block(at, _):
        row = pl.multiple_of(at * TILE, TILE)
        rows = [pl.ds(pl.multiple_of(row + c * TILE, TILE), TILE) for c in range(chunks + 1)]
        shift = [
            jnp.where(jnp.logical_and(first, at + c < chunks), -HIDDEN, 0.0) for c in range(chunks)
        ] + [0.0]
        queries, grads, probs, rounded, deltas = [], [], [], [], []
        for r in range(factor):
            q = qb[n, pl.ds(row, TILE), r * width : (r + 1) * width]
            g = gb[n, pl.ds(row, TILE), r * width : (r + 1) * width]
            scores = []
            for c in range(chunks + 1):
                s = matmul_nt(kb[n, rows[c], :], q)
                if c == 0:
                    s = jnp.where(key_at > query_at, s, HIDDEN)
                if c == chunks:
                    s = jnp.where(key_at <= query_at, s, HIDDEN)
                scores.append(s)
            top = None
            for c in range(chunks + 1):
                most = jnp.max(scores[c], axis=0, keepdims=True) - shift[c]
                top = most if top is None else jnp.maximum(top, most)
            total = None
            powers = []
            for c in range(chunks + 1):
                e = jnp.exp2(scores[c] * exponent_scale - (top + shift[c]) * exponent_scale)
                part = jnp.sum(e, axis=0, keepdims=True)
                total = part if total is None else total + part
                powers.append(e)
            inverse = 1.0 / total
            prob = [e * inverse for e in powers]
            prob_b = [p.astype(jnp.bfloat16) for p in prob]
            out = None
            for c in range(chunks + 1):
                part = matmul(vt[:, rows[c]], prob_b[c])
                out = part if out is None else out + part
            out_b = out.astype(jnp.bfloat16)
            deltas.append(jnp.sum(turned(g) * out_b.astype(jnp.float32), axis=0, keepdims=True))
            ob[n, pl.ds(row, TILE), r * width : (r + 1) * width] = out.T.astype(jnp.bfloat16)
            queries.append(q)
            grads.append(g)
            probs.append(prob)
            rounded.append(prob_b)
        dq = [None] * factor
        for c in range(chunks + 1):
            dk_part, dv_part = None, None
            for r in range(factor):
                dprob = matmul_nt(vb[n, rows[c], :], grads[r])
                ds = (probs[r][c] * (dprob - deltas[r])).astype(jnp.bfloat16)
                part = matmul(kt[:, rows[c]], ds)
                dq[r] = part if dq[r] is None else dq[r] + part
                part = matmul(ds, queries[r])
                dk_part = part if dk_part is None else dk_part + part
                part = matmul(rounded[r][c], grads[r])
                dv_part = part if dv_part is None else dv_part + part
            dk[n, rows[c], :] += dk_part
            dv[n, rows[c], :] += dv_part
        for r in range(factor):
            dqb[n, pl.ds(row, TILE), r * width : (r + 1) * width] = (dq[r] * query_scale).T.astype(jnp.bfloat16)
        return 0

    lax.fori_loop(0, (kb.shape[1] - WINDOW_TOKENS) // TILE, block, 0)


def kernel(
    near, heads, factor, queries, keys, values, cotangent, attended, grad_queries, key_gradient, value_gradient,
    qb, gb, kb, vb, kt, vt, ob, dqb, dk, dv, dk_far, dv_far, dk_back, dv_back, dk_own, dv_own,
    in_send, in_recv, halo_send, halo_recv, back_send, back_recv, out_send, out_recv,
):
    length = queries.shape[0]
    width = HEAD_SIZE
    side = lax.axis_size("head")
    members = near * side
    teams = lax.axis_size("seq") // near
    seq, head = lax.axis_index("seq"), lax.axis_index("head")
    team = seq // near
    me = lax.rem(seq, near) * side + head
    has_before, has_after = team > 0, team < teams - 1

    def device(team_at, member):
        return (team_at * near + member // side, lax.rem(member, side))

    ahead, behind = device(team + 1, me), device(team - 1, me)
    barrier = pltpu.get_barrier_semaphore()
    for d in range(1, members):
        pl.semaphore_signal(barrier, inc=1, device_id=device(team, lax.rem(me + d, members)), device_id_type=MESH)

    @pl.when(has_after)
    def _():
        pl.semaphore_signal(barrier, inc=1, device_id=ahead, device_id_type=MESH)

    @pl.when(has_before)
    def _():
        pl.semaphore_signal(barrier, inc=1, device_id=behind, device_id_type=MESH)

    pl.semaphore_wait(barrier, members - 1 + has_after.astype(jnp.int32) + has_before.astype(jnp.int32))

    def columns(member, n, size):
        return pl.ds(pl.multiple_of((member * heads + n) * size, size), size)

    def token_rows(member, start=0):
        return pl.ds(pl.multiple_of(start + member * length, length), length)

    wide = factor * width
    entering = ((keys, width, kb, WINDOW_TOKENS), (values, width, vb, WINDOW_TOKENS), (queries, wide, qb, 0), (cotangent, wide, gb, 0))
    leaving = ((ob, wide, attended), (dqb, wide, grad_queries), (dk_own, width, key_gradient), (dv_own, width, value_gradient))

    def entry(n, d, a):
        source, size, buffer, start = entering[a]
        other = lax.rem(me + d, members)
        src = source.at[:, columns(other, n, size)]
        dst = buffer.at[n, token_rows(me, start), :]
        if d == 0:
            return pltpu.make_async_copy(src, dst, in_recv.at[n, 0, a])
        return pltpu.make_async_remote_copy(
            src, dst, in_send.at[n, d, a], in_recv.at[n, d, a], device_id=device(team, other), device_id_type=MESH
        )

    def enter(n, which):
        for a in which:
            for d in (*range(1, members), 0):
                entry(n, d, a).start()

    def entered(n, which):
        for a in which:
            entry(n, 0, a).wait()
            for d in range(1, members):
                entry(n, d, a).wait_recv()

    def halo(n, a):
        buffer = entering[a][2]
        return pltpu.make_async_remote_copy(
            buffer.at[n, pl.ds(WINDOW_TOKENS, WINDOW_TOKENS), :], buffer.at[n, pl.ds(0, WINDOW_TOKENS), :],
            halo_send.at[n, a], halo_recv.at[n, a], device_id=ahead, device_id_type=MESH,
        )

    def back(n, a):
        source, target = ((dk_far, dk_back), (dv_far, dv_back))[a]
        return pltpu.make_async_remote_copy(
            source.at[n], target.at[n], back_send.at[n, a], back_recv.at[n, a], device_id=behind, device_id_type=MESH
        )

    def exit_copy(n, d, a):
        buffer, size, target = leaving[a]
        other = lax.rem(me + d, members)
        src = buffer.at[n, token_rows(other), :]
        dst = target.at[:, columns(me, n, size)]
        if d == 0:
            return pltpu.make_async_copy(src, dst, out_recv.at[n, 0, a])
        return pltpu.make_async_remote_copy(
            src, dst, out_send.at[n, d, a], out_recv.at[n, d, a], device_id=device(team, other), device_id_type=MESH
        )

    def leave(n, which):
        for a in which:
            for d in (*range(1, members), 0):
                exit_copy(n, d, a).start()

    def send_halo(n):
        entered(n, (0, 1))

        @pl.when(has_after)
        def _():
            halo(n, 0).start()
            halo(n, 1).start()

    def finish(n):
        for a, (total, received, result, factor_of) in enumerate(
            ((dk, dk_back, dk_own, query_scale), (dv, dv_back, dv_own, 1.0))
        ):
            own = total[n, pl.ds(WINDOW_TOKENS, WINDOW_TOKENS), :] * factor_of

            @pl.when(has_after)
            def _():
                back(n, a).wait_recv()
                result[n] = (own + received[n].astype(jnp.float32)).astype(jnp.bfloat16)

            @pl.when(jnp.logical_not(has_after))
            def _():
                result[n] = own.astype(jnp.bfloat16)

        leave(n, (2, 3))

    @pl.when(jnp.logical_not(has_before))
    def _():
        for n in range(heads):
            kb[n, pl.ds(0, WINDOW_TOKENS), :] = jnp.zeros((WINDOW_TOKENS, width), kb.dtype)
            vb[n, pl.ds(0, WINDOW_TOKENS), :] = jnp.zeros((WINDOW_TOKENS, width), vb.dtype)

    enter(0, (0, 1))
    if heads > 1:
        enter(1, (0, 1))
    enter(0, (2, 3))
    if heads > 2:
        enter(2, (0, 1))
    if heads > 1:
        enter(1, (2, 3))
    send_halo(0)

    def step(n, _):
        @pl.when(n + 1 < heads)
        def _():
            send_halo(n + 1)

        entered(n, (2, 3))

        @pl.when(n + 3 < heads)
        def _():
            enter(n + 3, (0, 1))

        @pl.when(n + 2 < heads)
        def _():
            enter(n + 2, (2, 3))

        @pl.when(has_before)
        def _():
            halo(n, 0).wait_recv()
            halo(n, 1).wait_recv()

        attend(n, factor, jnp.logical_not(has_before), qb, gb, kb, vb, kt, vt, ob, dqb, dk, dv)

        @pl.when(has_before)
        def _():
            dk_far[n] = (dk[n, pl.ds(0, WINDOW_TOKENS), :] * query_scale).astype(jnp.bfloat16)
            dv_far[n] = dv[n, pl.ds(0, WINDOW_TOKENS), :].astype(jnp.bfloat16)
            back(n, 0).start()
            back(n, 1).start()

        leave(n, (0, 1))

        @pl.when(n > 0)
        def _():
            finish(n - 1)

        return 0

    lax.fori_loop(0, heads, step, 0)
    finish(heads - 1)

    def drain(n, _):
        for a in range(4):
            exit_copy(n, 0, a).wait()
            for d in range(1, members):
                entry(n, d, a).wait_send()
                exit_copy(n, d, a).wait()

        @pl.when(has_after)
        def _():
            halo(n, 0).wait_send()
            halo(n, 1).wait_send()

        @pl.when(has_before)
        def _():
            back(n, 0).wait_send()
            back(n, 1).wait_send()

        return 0

    lax.fori_loop(0, heads, drain, 0)


def body(queries, keys, values, output_cotangent):
    length = queries.shape[0]
    side = lax.axis_size("head")
    near = WINDOW_TOKENS // (length * side)
    members = near * side
    width = HEAD_SIZE
    heads = keys.shape[1] // width // members
    factor = queries.shape[1] // keys.shape[1]
    wide = factor * width
    low, high = jnp.bfloat16, jnp.float32
    window = WINDOW_TOKENS
    pairs = heads * 2 * window * TILE * 6 * factor * width
    return tuple(
        pl.pallas_call(
            functools.partial(kernel, near, heads, factor),
            out_shape=[jax.ShapeDtypeStruct(x.shape, x.dtype) for x in (queries, queries, keys, values)],
            in_specs=[pl.BlockSpec(memory_space=pl.ANY)] * 4,
            out_specs=[pl.BlockSpec(memory_space=pl.ANY)] * 4,
            scratch_shapes=[
                pltpu.VMEM((heads, window, wide), low),
                pltpu.VMEM((heads, window, wide), low),
                pltpu.VMEM((heads, 2 * window, width), low),
                pltpu.VMEM((heads, 2 * window, width), low),
                pltpu.VMEM((width, 2 * window), low),
                pltpu.VMEM((width, 2 * window), low),
                pltpu.VMEM((heads, window, wide), low),
                pltpu.VMEM((heads, window, wide), low),
                pltpu.VMEM((heads, 2 * window, width), high),
                pltpu.VMEM((heads, 2 * window, width), high),
                *[pltpu.VMEM((heads, window, width), low)] * 6,
                pltpu.SemaphoreType.DMA((heads, members, 4)),
                pltpu.SemaphoreType.DMA((heads, members, 4)),
                *[pltpu.SemaphoreType.DMA((heads, 2))] * 4,
                pltpu.SemaphoreType.DMA((heads, members, 4)),
                pltpu.SemaphoreType.DMA((heads, members, 4)),
            ],
            compiler_params=pltpu.CompilerParams(
                collective_id=0, has_side_effects=True, vmem_limit_bytes=60 * 1024 * 1024
            ),
            cost_estimate=pl.CostEstimate(flops=pairs * 2, bytes_accessed=24 * queries.size, transcendentals=0),
        )(queries, keys, values, output_cotangent)
    )


def solution(mesh):
    spec = P(("seq", "head"), None)
    return jax.shard_map(
        body,
        mesh=mesh,
        in_specs=(spec,) * 4,
        out_specs=(spec,) * 4,
        check_vma=False,
    )
```

```python
import functools

import jax
import jax.numpy as jnp
from jax import lax
from jax.experimental import pallas as pl
from jax.experimental.pallas import tpu as pltpu
from jax.sharding import PartitionSpec as P

HEAD_SIZE = 128
WINDOW_TOKENS = 1024
TILE = 256
MESH = pl.DeviceIdType.MESH

query_scale = 168.0 ** (-0.5)
exponent_scale = query_scale * 1.4426950408889634
HIDDEN = -1e30


def matmul(left, right):
    return jnp.dot(left, right, preferred_element_type=jnp.float32)


def matmul_nt(left, right):
    return lax.dot_general(left, right, (((1,), (1,)), ((), ())), preferred_element_type=jnp.float32)


def turned(value):
    return value.astype(jnp.float32).T


def attend(n, factor, first, qb, gb, kb, vb, kt, vt, probs_b, dscores_b, ob, dqb, dk, dv, after_tile):
    width = HEAD_SIZE
    chunks = WINDOW_TOKENS // TILE
    span = WINDOW_TOKENS + TILE
    dk[n] = jnp.zeros(dk.shape[1:], jnp.float32)
    dv[n] = jnp.zeros(dv.shape[1:], jnp.float32)

    def turn(at, _):
        row = pl.multiple_of(at * TILE, TILE)
        kt[:, pl.ds(row, TILE)] = turned(kb[n, pl.ds(row, TILE), :]).astype(jnp.bfloat16)
        vt[:, pl.ds(row, TILE)] = turned(vb[n, pl.ds(row, TILE), :]).astype(jnp.bfloat16)
        return 0

    lax.fori_loop(0, kb.shape[1] // TILE, turn, 0)
    across = factor * TILE
    key_at = lax.broadcasted_iota(jnp.int32, (TILE, across), 0)
    query_at = lax.broadcasted_iota(jnp.int32, (TILE, across), 1) % TILE

    def block(at, _):
        row = pl.multiple_of(at * TILE, TILE)
        slab = pl.ds(row, span)
        rows = [pl.ds(pl.multiple_of(row + c * TILE, TILE), TILE) for c in range(chunks + 1)]
        shift = [
            jnp.where(jnp.logical_and(first, at + c < chunks), -HIDDEN, 0.0) for c in range(chunks)
        ] + [0.0]
        q = jnp.concatenate([qb[n, pl.ds(row, TILE), r * width : (r + 1) * width] for r in range(factor)], 0)
        g = jnp.concatenate([gb[n, pl.ds(row, TILE), r * width : (r + 1) * width] for r in range(factor)], 0)
        scores = []
        for c in range(chunks + 1):
            s = matmul_nt(kb[n, rows[c], :], q)
            if c == 0:
                s = jnp.where(key_at > query_at, s, HIDDEN)
            if c == chunks:
                s = jnp.where(key_at <= query_at, s, HIDDEN)
            scores.append(s)
        top = None
        for c in range(chunks + 1):
            most = jnp.max(scores[c], axis=0, keepdims=True) - shift[c]
            top = most if top is None else jnp.maximum(top, most)
        total = None
        powers = []
        for c in range(chunks + 1):
            e = jnp.exp2(scores[c] * exponent_scale - (top + shift[c]) * exponent_scale)
            part = jnp.sum(e, axis=0, keepdims=True)
            total = part if total is None else total + part
            powers.append(e)
        inverse = 1.0 / total
        probs = [e * inverse for e in powers]
        for c in range(chunks + 1):
            probs_b[c * TILE : (c + 1) * TILE, :] = probs[c].astype(jnp.bfloat16)
        out = matmul(vt[:, slab], probs_b[...])
        out_b = out.astype(jnp.bfloat16).astype(jnp.float32)
        delta = jnp.sum(turned(g) * out_b, axis=0, keepdims=True)
        for r in range(factor):
            ob[n, pl.ds(row, TILE), r * width : (r + 1) * width] = out[:, r * TILE : (r + 1) * TILE].T.astype(jnp.bfloat16)
        for c in range(chunks + 1):
            dprobs = matmul_nt(vb[n, rows[c], :], g)
            dscores_b[c * TILE : (c + 1) * TILE, :] = (probs[c] * (dprobs - delta)).astype(jnp.bfloat16)
        dq = matmul(kt[:, slab], dscores_b[...]) * query_scale
        for c in range(chunks + 1):
            dv[n, rows[c], :] += matmul(probs_b[c * TILE : (c + 1) * TILE, :], g)
            dk[n, rows[c], :] += matmul(dscores_b[c * TILE : (c + 1) * TILE, :], q)
        for r in range(factor):
            dqb[n, pl.ds(row, TILE), r * width : (r + 1) * width] = dq[:, r * TILE : (r + 1) * TILE].T.astype(jnp.bfloat16)
        after_tile(at)
        return 0

    lax.fori_loop(0, (kb.shape[1] - WINDOW_TOKENS) // TILE, block, 0)


def kernel(
    near, heads, factor, queries, keys, values, cotangent, attended, grad_queries, key_gradient, value_gradient,
    qb, gb, kb, vb, kt, vt, probs_b, dscores_b, ob, dqb, dk, dv, dk_far, dv_far, dk_back, dv_back, dk_own, dv_own,
    in_send, in_recv, halo_send, halo_recv, back_send, back_recv, out_send, out_recv,
):
    length = queries.shape[0]
    width = HEAD_SIZE
    side = lax.axis_size("head")
    members = near * side
    teams = lax.axis_size("seq") // near
    seq, head = lax.axis_index("seq"), lax.axis_index("head")
    team = seq // near
    me = lax.rem(seq, near) * side + head
    has_before, has_after = team > 0, team < teams - 1

    def device(team_at, member):
        return (team_at * near + member // side, lax.rem(member, side))

    ahead, behind = device(team + 1, me), device(team - 1, me)
    barrier = pltpu.get_barrier_semaphore()
    for d in range(1, members):
        pl.semaphore_signal(barrier, inc=1, device_id=device(team, lax.rem(me + d, members)), device_id_type=MESH)

    @pl.when(has_after)
    def _():
        pl.semaphore_signal(barrier, inc=1, device_id=ahead, device_id_type=MESH)

    @pl.when(has_before)
    def _():
        pl.semaphore_signal(barrier, inc=1, device_id=behind, device_id_type=MESH)

    pl.semaphore_wait(barrier, members - 1 + has_after.astype(jnp.int32) + has_before.astype(jnp.int32))

    def columns(member, n, size):
        return pl.ds(pl.multiple_of((member * heads + n) * size, size), size)

    def token_rows(member, start=0):
        return pl.ds(pl.multiple_of(start + member * length, length), length)

    wide = factor * width
    entering = ((keys, width, kb, WINDOW_TOKENS), (values, width, vb, WINDOW_TOKENS), (queries, wide, qb, 0), (cotangent, wide, gb, 0))
    leaving = ((ob, wide, attended), (dqb, wide, grad_queries), (dk_own, width, key_gradient), (dv_own, width, value_gradient))

    def entry(n, d, a):
        source, size, buffer, start = entering[a]
        other = lax.rem(me + d, members)
        src = source.at[:, columns(other, n, size)]
        dst = buffer.at[n, token_rows(me, start), :]
        if d == 0:
            return pltpu.make_async_copy(src, dst, in_recv.at[n, 0, a])
        return pltpu.make_async_remote_copy(
            src, dst, in_send.at[n, d, a], in_recv.at[n, d, a], device_id=device(team, other), device_id_type=MESH
        )

    def enter(n, which):
        for a in which:
            for d in (*range(1, members), 0):
                entry(n, d, a).start()

    def entered(n, which):
        for a in which:
            entry(n, 0, a).wait()
            for d in range(1, members):
                entry(n, d, a).wait_recv()

    def halo(n, a):
        buffer = entering[a][2]
        return pltpu.make_async_remote_copy(
            buffer.at[n, pl.ds(WINDOW_TOKENS, WINDOW_TOKENS), :], buffer.at[n, pl.ds(0, WINDOW_TOKENS), :],
            halo_send.at[n, a], halo_recv.at[n, a], device_id=ahead, device_id_type=MESH,
        )

    chunks = WINDOW_TOKENS // TILE

    def back(n, a, c):
        source, target = ((dk_far, dk_back), (dv_far, dv_back))[a]
        rows = pl.ds(pl.multiple_of(c * TILE, TILE), TILE)
        return pltpu.make_async_remote_copy(
            source.at[n, rows, :], target.at[n, rows, :], back_send.at[n, a, c], back_recv.at[n, a, c],
            device_id=behind, device_id_type=MESH,
        )

    def exit_own(n, a):
        buffer, size, target = leaving[a]
        return pltpu.make_async_copy(
            buffer.at[n, token_rows(me), :], target.at[:, columns(me, n, size)], out_recv.at[n, 0, a]
        )

    def exit_copy(n, d, a):
        buffer, size, target = leaving[a]
        other = lax.rem(me + d, members)
        return pltpu.make_async_remote_copy(
            buffer.at[n, token_rows(other), :], target.at[:, columns(me, n, size)],
            out_send.at[n, d, a], out_recv.at[n, d, a], device_id=device(team, other), device_id_type=MESH,
        )

    def leave(n, which):
        for a in which:
            for d in range(1, members):
                exit_copy(n, d, a).start()
            exit_own(n, a).start()

    def send_halo(n):
        entered(n, (0, 1))

        @pl.when(has_after)
        def _():
            halo(n, 0).start()
            halo(n, 1).start()

    def finish(n):
        for a, (total, received, result, factor_of) in enumerate(
            ((dk, dk_back, dk_own, query_scale), (dv, dv_back, dv_own, 1.0))
        ):
            own = total[n, pl.ds(WINDOW_TOKENS, WINDOW_TOKENS), :] * factor_of

            @pl.when(has_after)
            def _():
                for c in range(chunks):
                    back(n, a, c).wait_recv()
                result[n] = (own + received[n].astype(jnp.float32)).astype(jnp.bfloat16)

            @pl.when(jnp.logical_not(has_after))
            def _():
                result[n] = own.astype(jnp.bfloat16)

        leave(n, (2, 3))

    @pl.when(jnp.logical_not(has_before))
    def _():
        for n in range(heads):
            kb[n, pl.ds(0, WINDOW_TOKENS), :] = jnp.zeros((WINDOW_TOKENS, width), kb.dtype)
            vb[n, pl.ds(0, WINDOW_TOKENS), :] = jnp.zeros((WINDOW_TOKENS, width), vb.dtype)

    enter(0, (0, 1))
    if heads > 1:
        enter(1, (0, 1))
    enter(0, (2, 3))
    if heads > 2:
        enter(2, (0, 1))
    if heads > 1:
        enter(1, (2, 3))
    send_halo(0)

    def step(n, _):
        @pl.when(n + 1 < heads)
        def _():
            send_halo(n + 1)

        entered(n, (2, 3))

        @pl.when(n + 3 < heads)
        def _():
            enter(n + 3, (0, 1))

        @pl.when(n + 2 < heads)
        def _():
            enter(n + 2, (2, 3))

        @pl.when(has_before)
        def _():
            halo(n, 0).wait_recv()
            halo(n, 1).wait_recv()

        def after_tile(at):
            @pl.when(has_before)
            def _():
                rows = pl.ds(pl.multiple_of(at * TILE, TILE), TILE)
                dk_far[n, rows, :] = (dk[n, rows, :] * query_scale).astype(jnp.bfloat16)
                dv_far[n, rows, :] = dv[n, rows, :].astype(jnp.bfloat16)
                back(n, 0, at).start()
                back(n, 1, at).start()

            for m in range(TILE // length):
                d = lax.rem(at * (TILE // length) + m - me + members, members)

                @pl.when(d == 0)
                def _():
                    exit_own(n, 0).start()
                    exit_own(n, 1).start()

                @pl.when(d > 0)
                def _():
                    exit_copy(n, d, 0).start()
                    exit_copy(n, d, 1).start()

        attend(
            n, factor, jnp.logical_not(has_before), qb, gb, kb, vb, kt, vt, probs_b, dscores_b, ob, dqb, dk, dv, after_tile
        )

        @pl.when(n > 0)
        def _():
            finish(n - 1)

        return 0

    lax.fori_loop(0, heads, step, 0)
    finish(heads - 1)

    def drain(n, _):
        for a in range(4):
            exit_own(n, a).wait()
            for d in range(1, members):
                entry(n, d, a).wait_send()
                exit_copy(n, d, a).wait()

        @pl.when(has_after)
        def _():
            halo(n, 0).wait_send()
            halo(n, 1).wait_send()

        @pl.when(has_before)
        def _():
            for c in range(chunks):
                back(n, 0, c).wait_send()
                back(n, 1, c).wait_send()

        return 0

    lax.fori_loop(0, heads, drain, 0)


def hand_over(*refs):
    sources, targets, sems = refs[:4], refs[4:8], refs[8]
    parts = sems.shape[1]
    copies = []
    for a in range(4):
        rows = sources[a].shape[0] // parts
        for p in range(parts):
            piece = pl.ds(p * rows, rows)
            copies.append(pltpu.make_async_copy(sources[a].at[piece, :], targets[a].at[piece, :], sems.at[a, p]))
    for copy in copies:
        copy.start()
    for copy in copies:
        copy.wait()


def body(queries, keys, values, output_cotangent):
    length = queries.shape[0]
    side = lax.axis_size("head")
    near = WINDOW_TOKENS // (length * side)
    members = near * side
    width = HEAD_SIZE
    heads = keys.shape[1] // width // members
    factor = queries.shape[1] // keys.shape[1]
    wide = factor * width
    low, high = jnp.bfloat16, jnp.float32
    window = WINDOW_TOKENS
    pairs = heads * 2 * window * TILE * 6 * factor * width
    results = pl.pallas_call(
        functools.partial(kernel, near, heads, factor),
        out_shape=[jax.ShapeDtypeStruct(x.shape, x.dtype) for x in (queries, queries, keys, values)],
        in_specs=[pl.BlockSpec(memory_space=pl.ANY)] * 4,
        out_specs=[pl.BlockSpec(memory_space=pl.ANY)] * 4,
        scratch_shapes=[
            pltpu.VMEM((heads, window, wide), low),
            pltpu.VMEM((heads, window, wide), low),
            pltpu.VMEM((heads, 2 * window, width), low),
            pltpu.VMEM((heads, 2 * window, width), low),
            pltpu.VMEM((width, 2 * window), low),
            pltpu.VMEM((width, 2 * window), low),
            pltpu.VMEM((window + TILE, factor * TILE), low),
            pltpu.VMEM((window + TILE, factor * TILE), low),
            pltpu.VMEM((heads, window, wide), low),
            pltpu.VMEM((heads, window, wide), low),
            pltpu.VMEM((heads, 2 * window, width), high),
            pltpu.VMEM((heads, 2 * window, width), high),
            *[pltpu.VMEM((heads, window, width), low)] * 6,
            pltpu.SemaphoreType.DMA((heads, members, 4)),
            pltpu.SemaphoreType.DMA((heads, members, 4)),
            *[pltpu.SemaphoreType.DMA((heads, 2))] * 2,
            *[pltpu.SemaphoreType.DMA((heads, 2, window // TILE))] * 2,
            pltpu.SemaphoreType.DMA((heads, members, 4)),
            pltpu.SemaphoreType.DMA((heads, members, 4)),
        ],
        compiler_params=pltpu.CompilerParams(
            collective_id=0, has_side_effects=True, vmem_limit_bytes=60 * 1024 * 1024
        ),
        cost_estimate=pl.CostEstimate(flops=pairs * 2, bytes_accessed=24 * queries.size, transcendentals=0),
    )(queries, keys, values, output_cotangent)
    return tuple(
        pl.pallas_call(
            hand_over,
            out_shape=[jax.ShapeDtypeStruct(x.shape, x.dtype) for x in results],
            in_specs=[pl.BlockSpec(memory_space=pl.ANY)] * 4,
            out_specs=[pl.BlockSpec(memory_space=pl.ANY)] * 4,
            scratch_shapes=[pltpu.SemaphoreType.DMA((4, 4))],
            compiler_params=pltpu.CompilerParams(vmem_limit_bytes=60 * 1024 * 1024),
        )(*results)
    )


def solution(mesh):
    spec = P(("seq", "head"), None)
    return jax.shard_map(
        body,
        mesh=mesh,
        in_specs=(spec,) * 4,
        out_specs=(spec,) * 4,
        check_vma=False,
    )
```

```python
import functools

import jax
import jax.numpy as jnp
from jax import lax
from jax.experimental import pallas as pl
from jax.experimental.pallas import tpu as pltpu
from jax.sharding import PartitionSpec as P

HEAD_SIZE = 128
WINDOW_TOKENS = 1024
TILE = 256
MESH = pl.DeviceIdType.MESH

query_scale = 168.0 ** (-0.5)
exponent_scale = query_scale * 1.4426950408889634
HIDDEN = -1e30


def matmul(left, right):
    return jnp.dot(left, right, preferred_element_type=jnp.float32)


def matmul_nt(left, right):
    return lax.dot_general(left, right, (((1,), (1,)), ((), ())), preferred_element_type=jnp.float32)


def turned(value):
    return value.astype(jnp.float32).T


def attend(n, factor, first, qb, gb, kb, vb, kt, vt, probs_b, dscores_b, ob, dqb, dk, dv, after_tile):
    width = HEAD_SIZE
    chunks = WINDOW_TOKENS // TILE
    span = WINDOW_TOKENS + TILE
    dk[n] = jnp.zeros(dk.shape[1:], jnp.float32)
    dv[n] = jnp.zeros(dv.shape[1:], jnp.float32)

    def turn(at, _):
        row = pl.multiple_of(at * TILE, TILE)
        kt[:, pl.ds(row, TILE)] = turned(kb[n, pl.ds(row, TILE), :]).astype(jnp.bfloat16)
        vt[:, pl.ds(row, TILE)] = turned(vb[n, pl.ds(row, TILE), :]).astype(jnp.bfloat16)
        return 0

    lax.fori_loop(0, kb.shape[1] // TILE, turn, 0)
    across = factor * TILE
    key_at = lax.broadcasted_iota(jnp.int32, (TILE, across), 0)
    query_at = lax.broadcasted_iota(jnp.int32, (TILE, across), 1) % TILE

    def block(at, spot):
        row = pl.multiple_of(at * TILE, TILE)
        slab = pl.ds(row, span)
        rows = [pl.ds(pl.multiple_of(row + c * TILE, TILE), TILE) for c in range(chunks + 1)]
        here = [slice(c * TILE, (c + 1) * TILE) for c in range(chunks + 1)]
        shift = [
            jnp.where(jnp.logical_and(first, at + c < chunks), -HIDDEN, 0.0) for c in range(chunks)
        ] + [0.0]
        q = jnp.concatenate([qb[n, pl.ds(row, TILE), r * width : (r + 1) * width] for r in range(factor)], 0)
        g = jnp.concatenate([gb[n, pl.ds(row, TILE), r * width : (r + 1) * width] for r in range(factor)], 0)
        scores = []
        top = None
        for c in range(chunks + 1):
            s = matmul_nt(kb[n, rows[c], :], q)
            if c == 0:
                s = jnp.where(key_at > query_at, s, HIDDEN)
            if c == chunks:
                s = jnp.where(key_at <= query_at, s, HIDDEN)
            scores.append(s)
            most = jnp.max(s, axis=0, keepdims=True) - shift[c]
            top = most if top is None else jnp.maximum(top, most)
        total = None
        powers, dprobs = [], []
        for c in range(chunks + 1):
            dprobs.append(matmul_nt(vb[n, rows[c], :], g))
            e = jnp.exp2(scores[c] * exponent_scale - (top + shift[c]) * exponent_scale)
            part = jnp.sum(e, axis=0, keepdims=True)
            total = part if total is None else total + part
            powers.append(e)
        inverse = 1.0 / total
        probs = []
        for c in range(chunks + 1):
            probs.append(powers[c] * inverse)
            probs_b[spot, here[c], :] = probs[c].astype(jnp.bfloat16)
        out = matmul(vt[:, slab], probs_b[spot])
        out_b = out.astype(jnp.bfloat16).astype(jnp.float32)
        delta = jnp.sum(turned(g) * out_b, axis=0, keepdims=True)
        for r in range(factor):
            ob[n, pl.ds(row, TILE), r * width : (r + 1) * width] = out[:, r * TILE : (r + 1) * TILE].T.astype(jnp.bfloat16)
        for c in range(chunks + 1):
            dscores_b[spot, here[c], :] = (probs[c] * (dprobs[c] - delta)).astype(jnp.bfloat16)
            dv[n, rows[c], :] += matmul(probs_b[spot, here[c], :], g)
        dq = matmul(kt[:, slab], dscores_b[spot]) * query_scale
        for c in range(chunks + 1):
            dk[n, rows[c], :] += matmul(dscores_b[spot, here[c], :], q)
        for r in range(factor):
            dqb[n, pl.ds(row, TILE), r * width : (r + 1) * width] = dq[:, r * TILE : (r + 1) * TILE].T.astype(jnp.bfloat16)

    def pair(at, _):
        block(2 * at, 0)
        block(2 * at + 1, 1)
        after_tile(2 * at)
        after_tile(2 * at + 1)
        return 0

    lax.fori_loop(0, WINDOW_TOKENS // TILE // 2, pair, 0)


def kernel(
    near, heads, factor, queries, keys, values, cotangent, attended, grad_queries, key_gradient, value_gradient,
    qb, gb, kb, vb, kt, vt, probs_b, dscores_b, ob, dqb, dk, dv, dk_far, dv_far, dk_back, dv_back, dk_own, dv_own,
    in_send, in_recv, halo_send, halo_recv, back_send, back_recv, out_send, out_recv,
):
    length = queries.shape[0]
    width = HEAD_SIZE
    side = lax.axis_size("head")
    members = near * side
    teams = lax.axis_size("seq") // near
    seq, head = lax.axis_index("seq"), lax.axis_index("head")
    team = seq // near
    me = lax.rem(seq, near) * side + head
    has_before, has_after = team > 0, team < teams - 1

    def device(team_at, member):
        return (team_at * near + member // side, lax.rem(member, side))

    ahead, behind = device(team + 1, me), device(team - 1, me)
    barrier = pltpu.get_barrier_semaphore()
    for d in range(1, members):
        pl.semaphore_signal(barrier, inc=1, device_id=device(team, lax.rem(me + d, members)), device_id_type=MESH)

    @pl.when(has_after)
    def _():
        pl.semaphore_signal(barrier, inc=1, device_id=ahead, device_id_type=MESH)

    @pl.when(has_before)
    def _():
        pl.semaphore_signal(barrier, inc=1, device_id=behind, device_id_type=MESH)

    pl.semaphore_wait(barrier, members - 1 + has_after.astype(jnp.int32) + has_before.astype(jnp.int32))

    def columns(member, n, size):
        return pl.ds(pl.multiple_of((member * heads + n) * size, size), size)

    def token_rows(member, start=0):
        return pl.ds(pl.multiple_of(start + member * length, length), length)

    wide = factor * width
    entering = ((keys, width, kb, WINDOW_TOKENS), (values, width, vb, WINDOW_TOKENS), (queries, wide, qb, 0), (cotangent, wide, gb, 0))
    leaving = ((ob, wide, attended), (dqb, wide, grad_queries), (dk_own, width, key_gradient), (dv_own, width, value_gradient))

    def entry(n, d, a):
        source, size, buffer, start = entering[a]
        other = lax.rem(me + d, members)
        src = source.at[:, columns(other, n, size)]
        dst = buffer.at[n, token_rows(me, start), :]
        if d == 0:
            return pltpu.make_async_copy(src, dst, in_recv.at[n, 0, a])
        return pltpu.make_async_remote_copy(
            src, dst, in_send.at[n, d, a], in_recv.at[n, d, a], device_id=device(team, other), device_id_type=MESH
        )

    def enter(n, which):
        for a in which:
            for d in (*range(1, members), 0):
                entry(n, d, a).start()

    def entered(n, which):
        for a in which:
            entry(n, 0, a).wait()
            for d in range(1, members):
                entry(n, d, a).wait_recv()

    def halo(n, a):
        buffer = entering[a][2]
        return pltpu.make_async_remote_copy(
            buffer.at[n, pl.ds(WINDOW_TOKENS, WINDOW_TOKENS), :], buffer.at[n, pl.ds(0, WINDOW_TOKENS), :],
            halo_send.at[n, a], halo_recv.at[n, a], device_id=ahead, device_id_type=MESH,
        )

    chunks = WINDOW_TOKENS // TILE

    def back(n, a, c):
        source, target = ((dk_far, dk_back), (dv_far, dv_back))[a]
        rows = pl.ds(pl.multiple_of(c * TILE, TILE), TILE)
        return pltpu.make_async_remote_copy(
            source.at[n, rows, :], target.at[n, rows, :], back_send.at[n, a, c], back_recv.at[n, a, c],
            device_id=behind, device_id_type=MESH,
        )

    def exit_own(n, a):
        buffer, size, target = leaving[a]
        return pltpu.make_async_copy(
            buffer.at[n, token_rows(me), :], target.at[:, columns(me, n, size)], out_recv.at[n, 0, a]
        )

    def exit_copy(n, d, a):
        buffer, size, target = leaving[a]
        other = lax.rem(me + d, members)
        return pltpu.make_async_remote_copy(
            buffer.at[n, token_rows(other), :], target.at[:, columns(me, n, size)],
            out_send.at[n, d, a], out_recv.at[n, d, a], device_id=device(team, other), device_id_type=MESH,
        )

    def leave(n, which):
        for a in which:
            for d in range(1, members):
                exit_copy(n, d, a).start()
            exit_own(n, a).start()

    def send_halo(n):
        entered(n, (0, 1))

        @pl.when(has_after)
        def _():
            halo(n, 0).start()
            halo(n, 1).start()

    def finish(n):
        for a, (total, received, result, factor_of) in enumerate(
            ((dk, dk_back, dk_own, query_scale), (dv, dv_back, dv_own, 1.0))
        ):
            own = total[n, pl.ds(WINDOW_TOKENS, WINDOW_TOKENS), :] * factor_of

            @pl.when(has_after)
            def _():
                for c in range(chunks):
                    back(n, a, c).wait_recv()
                result[n] = (own + received[n].astype(jnp.float32)).astype(jnp.bfloat16)

            @pl.when(jnp.logical_not(has_after))
            def _():
                result[n] = own.astype(jnp.bfloat16)

        leave(n, (2, 3))

    @pl.when(jnp.logical_not(has_before))
    def _():
        for n in range(heads):
            kb[n, pl.ds(0, WINDOW_TOKENS), :] = jnp.zeros((WINDOW_TOKENS, width), kb.dtype)
            vb[n, pl.ds(0, WINDOW_TOKENS), :] = jnp.zeros((WINDOW_TOKENS, width), vb.dtype)

    enter(0, (0, 1))
    if heads > 1:
        enter(1, (0, 1))
    enter(0, (2, 3))
    if heads > 2:
        enter(2, (0, 1))
    if heads > 1:
        enter(1, (2, 3))
    send_halo(0)

    def step(n, _):
        @pl.when(n + 1 < heads)
        def _():
            send_halo(n + 1)

        entered(n, (2, 3))

        @pl.when(n + 3 < heads)
        def _():
            enter(n + 3, (0, 1))

        @pl.when(n + 2 < heads)
        def _():
            enter(n + 2, (2, 3))

        @pl.when(has_before)
        def _():
            halo(n, 0).wait_recv()
            halo(n, 1).wait_recv()

        def after_tile(at):
            @pl.when(has_before)
            def _():
                rows = pl.ds(pl.multiple_of(at * TILE, TILE), TILE)
                dk_far[n, rows, :] = (dk[n, rows, :] * query_scale).astype(jnp.bfloat16)
                dv_far[n, rows, :] = dv[n, rows, :].astype(jnp.bfloat16)
                back(n, 0, at).start()
                back(n, 1, at).start()

            for m in range(TILE // length):
                d = lax.rem(at * (TILE // length) + m - me + members, members)

                @pl.when(d == 0)
                def _():
                    exit_own(n, 0).start()
                    exit_own(n, 1).start()

                @pl.when(d > 0)
                def _():
                    exit_copy(n, d, 0).start()
                    exit_copy(n, d, 1).start()

        attend(
            n, factor, jnp.logical_not(has_before), qb, gb, kb, vb, kt, vt, probs_b, dscores_b, ob, dqb, dk, dv, after_tile
        )

        @pl.when(n > 0)
        def _():
            finish(n - 1)

        return 0

    lax.fori_loop(0, heads, step, 0)
    finish(heads - 1)

    def drain(n, _):
        for a in range(4):
            exit_own(n, a).wait()
            for d in range(1, members):
                entry(n, d, a).wait_send()
                exit_copy(n, d, a).wait()

        @pl.when(has_after)
        def _():
            halo(n, 0).wait_send()
            halo(n, 1).wait_send()

        @pl.when(has_before)
        def _():
            for c in range(chunks):
                back(n, 0, c).wait_send()
                back(n, 1, c).wait_send()

        return 0

    lax.fori_loop(0, heads, drain, 0)


def hand_over(*refs):
    for source, target in zip(refs[:4], refs[4:]):
        target[...] = source[...]


def body(queries, keys, values, output_cotangent):
    length = queries.shape[0]
    side = lax.axis_size("head")
    near = WINDOW_TOKENS // (length * side)
    members = near * side
    width = HEAD_SIZE
    heads = keys.shape[1] // width // members
    factor = queries.shape[1] // keys.shape[1]
    wide = factor * width
    low, high = jnp.bfloat16, jnp.float32
    window = WINDOW_TOKENS
    pairs = heads * 2 * window * TILE * 6 * factor * width
    results = pl.pallas_call(
        functools.partial(kernel, near, heads, factor),
        out_shape=[jax.ShapeDtypeStruct(x.shape, x.dtype) for x in (queries, queries, keys, values)],
        in_specs=[pl.BlockSpec(memory_space=pl.ANY)] * 4,
        out_specs=[pl.BlockSpec(memory_space=pl.ANY)] * 4,
        scratch_shapes=[
            pltpu.VMEM((heads, window, wide), low),
            pltpu.VMEM((heads, window, wide), low),
            pltpu.VMEM((heads, 2 * window, width), low),
            pltpu.VMEM((heads, 2 * window, width), low),
            pltpu.VMEM((width, 2 * window), low),
            pltpu.VMEM((width, 2 * window), low),
            pltpu.VMEM((2, window + TILE, factor * TILE), low),
            pltpu.VMEM((2, window + TILE, factor * TILE), low),
            pltpu.VMEM((heads, window, wide), low),
            pltpu.VMEM((heads, window, wide), low),
            pltpu.VMEM((heads, 2 * window, width), high),
            pltpu.VMEM((heads, 2 * window, width), high),
            *[pltpu.VMEM((heads, window, width), low)] * 6,
            pltpu.SemaphoreType.DMA((heads, members, 4)),
            pltpu.SemaphoreType.DMA((heads, members, 4)),
            *[pltpu.SemaphoreType.DMA((heads, 2))] * 2,
            *[pltpu.SemaphoreType.DMA((heads, 2, window // TILE))] * 2,
            pltpu.SemaphoreType.DMA((heads, members, 4)),
            pltpu.SemaphoreType.DMA((heads, members, 4)),
        ],
        compiler_params=pltpu.CompilerParams(
            collective_id=0, has_side_effects=True, vmem_limit_bytes=60 * 1024 * 1024
        ),
        cost_estimate=pl.CostEstimate(flops=pairs * 2, bytes_accessed=24 * queries.size, transcendentals=0),
    )(queries, keys, values, output_cotangent)
    return tuple(
        pl.pallas_call(
            hand_over,
            grid=(4,),
            out_shape=[jax.ShapeDtypeStruct(x.shape, x.dtype) for x in results],
            in_specs=[pl.BlockSpec((x.shape[0] // 4, x.shape[1]), lambda i: (i, 0)) for x in results],
            out_specs=[pl.BlockSpec((x.shape[0] // 4, x.shape[1]), lambda i: (i, 0)) for x in results],
            compiler_params=pltpu.CompilerParams(vmem_limit_bytes=60 * 1024 * 1024),
        )(*results)
    )


def solution(mesh):
    spec = P(("seq", "head"), None)
    return jax.shard_map(
        body,
        mesh=mesh,
        in_specs=(spec,) * 4,
        out_specs=(spec,) * 4,
        check_vma=False,
    )
```

```python
import functools

import jax
import jax.numpy as jnp
from jax import lax
from jax.experimental import pallas as pl
from jax.experimental.pallas import tpu as pltpu
from jax.sharding import PartitionSpec as P

HEAD_SIZE = 128
WINDOW_TOKENS = 1024
TILE = 256
MESH = pl.DeviceIdType.MESH

query_scale = 168.0 ** (-0.5)
exponent_scale = query_scale * 1.4426950408889634
HIDDEN = -1e30


def matmul(left, right):
    return jnp.dot(left, right, preferred_element_type=jnp.float32)


def matmul_nt(left, right):
    return lax.dot_general(left, right, (((1,), (1,)), ((), ())), preferred_element_type=jnp.float32)


def turned(value):
    return value.astype(jnp.float32).T


def attend(n, factor, first, qb, gb, kb, vb, kt, vt, probs_b, dscores_b, ob, dqb, dk, dv, after_tile):
    width = HEAD_SIZE
    chunks = WINDOW_TOKENS // TILE
    span = WINDOW_TOKENS + TILE
    dk[n] = jnp.zeros(dk.shape[1:], jnp.float32)
    dv[n] = jnp.zeros(dv.shape[1:], jnp.float32)

    def turn(at, _):
        row = pl.multiple_of(at * TILE, TILE)
        kt[:, pl.ds(row, TILE)] = turned(kb[n, pl.ds(row, TILE), :]).astype(jnp.bfloat16)
        vt[:, pl.ds(row, TILE)] = turned(vb[n, pl.ds(row, TILE), :]).astype(jnp.bfloat16)
        return 0

    lax.fori_loop(0, kb.shape[1] // TILE, turn, 0)
    across = factor * TILE
    key_at = lax.broadcasted_iota(jnp.int32, (TILE, across), 0)
    query_at = lax.broadcasted_iota(jnp.int32, (TILE, across), 1) % TILE

    def block(at, spot):
        row = pl.multiple_of(at * TILE, TILE)
        slab = pl.ds(row, span)
        rows = [pl.ds(pl.multiple_of(row + c * TILE, TILE), TILE) for c in range(chunks + 1)]
        here = [slice(c * TILE, (c + 1) * TILE) for c in range(chunks + 1)]
        shift = [
            jnp.where(jnp.logical_and(first, at + c < chunks), -HIDDEN, 0.0) for c in range(chunks)
        ] + [0.0]
        q = jnp.concatenate([qb[n, pl.ds(row, TILE), r * width : (r + 1) * width] for r in range(factor)], 0)
        g = jnp.concatenate([gb[n, pl.ds(row, TILE), r * width : (r + 1) * width] for r in range(factor)], 0)
        scores = []
        top = None
        for c in range(chunks + 1):
            s = matmul_nt(kb[n, rows[c], :], q)
            if c == 0:
                s = jnp.where(key_at > query_at, s, HIDDEN)
            if c == chunks:
                s = jnp.where(key_at <= query_at, s, HIDDEN)
            scores.append(s)
            most = jnp.max(s, axis=0, keepdims=True) - shift[c]
            top = most if top is None else jnp.maximum(top, most)
        total = None
        powers, dprobs = [], []
        for c in range(chunks + 1):
            dprobs.append(matmul_nt(vb[n, rows[c], :], g))
            e = jnp.exp2(scores[c] * exponent_scale - (top + shift[c]) * exponent_scale)
            part = jnp.sum(e, axis=0, keepdims=True)
            total = part if total is None else total + part
            powers.append(e)
        inverse = 1.0 / total
        probs = []
        for c in range(chunks + 1):
            probs.append(powers[c] * inverse)
            probs_b[spot, here[c], :] = probs[c].astype(jnp.bfloat16)
        out = matmul(vt[:, slab], probs_b[spot])
        out_b = out.astype(jnp.bfloat16).astype(jnp.float32)
        delta = jnp.sum(turned(g) * out_b, axis=0, keepdims=True)
        for r in range(factor):
            ob[n, pl.ds(row, TILE), r * width : (r + 1) * width] = out[:, r * TILE : (r + 1) * TILE].T.astype(jnp.bfloat16)
        for c in range(chunks + 1):
            dscores_b[spot, here[c], :] = (probs[c] * (dprobs[c] - delta)).astype(jnp.bfloat16)
            dv[n, rows[c], :] += matmul(probs_b[spot, here[c], :], g)
        dq = matmul(kt[:, slab], dscores_b[spot]) * query_scale
        for c in range(chunks + 1):
            dk[n, rows[c], :] += matmul(dscores_b[spot, here[c], :], q)
        for r in range(factor):
            dqb[n, pl.ds(row, TILE), r * width : (r + 1) * width] = dq[:, r * TILE : (r + 1) * TILE].T.astype(jnp.bfloat16)

    def tile(at, _):
        block(at, 0)
        after_tile(at)
        return 0

    lax.fori_loop(0, WINDOW_TOKENS // TILE, tile, 0)


def kernel(
    near, heads, factor, queries, keys, values, cotangent, attended, grad_queries, key_gradient, value_gradient,
    qb, gb, kb, vb, kt, vt, probs_b, dscores_b, ob, dqb, dk, dv, dk_far, dv_far, dk_back, dv_back, dk_own, dv_own,
    in_send, in_recv, halo_send, halo_recv, back_send, back_recv, out_send, out_recv,
):
    length = queries.shape[0]
    width = HEAD_SIZE
    side = lax.axis_size("head")
    members = near * side
    teams = lax.axis_size("seq") // near
    seq, head = lax.axis_index("seq"), lax.axis_index("head")
    team = seq // near
    me = lax.rem(seq, near) * side + head
    has_before, has_after = team > 0, team < teams - 1

    def device(team_at, member):
        return (team_at * near + member // side, lax.rem(member, side))

    ahead, behind = device(team + 1, me), device(team - 1, me)
    barrier = pltpu.get_barrier_semaphore()
    for d in range(1, members):
        pl.semaphore_signal(barrier, inc=1, device_id=device(team, lax.rem(me + d, members)), device_id_type=MESH)

    @pl.when(has_after)
    def _():
        pl.semaphore_signal(barrier, inc=1, device_id=ahead, device_id_type=MESH)

    @pl.when(has_before)
    def _():
        pl.semaphore_signal(barrier, inc=1, device_id=behind, device_id_type=MESH)

    pl.semaphore_wait(barrier, members - 1 + has_after.astype(jnp.int32) + has_before.astype(jnp.int32))

    def columns(member, n, size):
        return pl.ds(pl.multiple_of((member * heads + n) * size, size), size)

    def token_rows(member, start=0):
        return pl.ds(pl.multiple_of(start + member * length, length), length)

    wide = factor * width
    entering = ((keys, width, kb, WINDOW_TOKENS), (values, width, vb, WINDOW_TOKENS), (queries, wide, qb, 0), (cotangent, wide, gb, 0))
    leaving = ((ob, wide, attended), (dqb, wide, grad_queries), (dk_own, width, key_gradient), (dv_own, width, value_gradient))

    def entry(n, d, a):
        source, size, buffer, start = entering[a]
        other = lax.rem(me + d, members)
        src = source.at[:, columns(other, n, size)]
        dst = buffer.at[n, token_rows(me, start), :]
        if d == 0:
            return pltpu.make_async_copy(src, dst, in_recv.at[n, 0, a])
        return pltpu.make_async_remote_copy(
            src, dst, in_send.at[n, d, a], in_recv.at[n, d, a], device_id=device(team, other), device_id_type=MESH
        )

    def enter(n, which):
        for a in which:
            for d in (*range(1, members), 0):
                entry(n, d, a).start()

    def entered(n, which):
        for a in which:
            entry(n, 0, a).wait()
            for d in range(1, members):
                entry(n, d, a).wait_recv()

    def halo(n, a):
        buffer = entering[a][2]
        return pltpu.make_async_remote_copy(
            buffer.at[n, pl.ds(WINDOW_TOKENS, WINDOW_TOKENS), :], buffer.at[n, pl.ds(0, WINDOW_TOKENS), :],
            halo_send.at[n, a], halo_recv.at[n, a], device_id=ahead, device_id_type=MESH,
        )

    chunks = WINDOW_TOKENS // TILE

    def back(n, a, c):
        source, target = ((dk_far, dk_back), (dv_far, dv_back))[a]
        rows = pl.ds(pl.multiple_of(c * TILE, TILE), TILE)
        return pltpu.make_async_remote_copy(
            source.at[n, rows, :], target.at[n, rows, :], back_send.at[n, a, c], back_recv.at[n, a, c],
            device_id=behind, device_id_type=MESH,
        )

    def exit_own(n, a):
        buffer, size, target = leaving[a]
        return pltpu.make_async_copy(
            buffer.at[n, token_rows(me), :], target.at[:, columns(me, n, size)], out_recv.at[n, 0, a]
        )

    def exit_copy(n, d, a):
        buffer, size, target = leaving[a]
        other = lax.rem(me + d, members)
        return pltpu.make_async_remote_copy(
            buffer.at[n, token_rows(other), :], target.at[:, columns(me, n, size)],
            out_send.at[n, d, a], out_recv.at[n, d, a], device_id=device(team, other), device_id_type=MESH,
        )

    def leave(n, which):
        for a in which:
            for d in range(1, members):
                exit_copy(n, d, a).start()
            exit_own(n, a).start()

    def send_halo(n):
        entered(n, (0, 1))

        @pl.when(has_after)
        def _():
            halo(n, 0).start()
            halo(n, 1).start()

    def finish(n):
        for a, (total, received, result, factor_of) in enumerate(
            ((dk, dk_back, dk_own, query_scale), (dv, dv_back, dv_own, 1.0))
        ):
            own = total[n, pl.ds(WINDOW_TOKENS, WINDOW_TOKENS), :] * factor_of

            @pl.when(has_after)
            def _():
                for c in range(chunks):
                    back(n, a, c).wait_recv()
                result[n] = (own + received[n].astype(jnp.float32)).astype(jnp.bfloat16)

            @pl.when(jnp.logical_not(has_after))
            def _():
                result[n] = own.astype(jnp.bfloat16)

        leave(n, (2, 3))

    @pl.when(jnp.logical_not(has_before))
    def _():
        for n in range(heads):
            kb[n, pl.ds(0, WINDOW_TOKENS), :] = jnp.zeros((WINDOW_TOKENS, width), kb.dtype)
            vb[n, pl.ds(0, WINDOW_TOKENS), :] = jnp.zeros((WINDOW_TOKENS, width), vb.dtype)

    enter(0, (0, 1))
    if heads > 1:
        enter(1, (0, 1))
    enter(0, (2, 3))
    if heads > 2:
        enter(2, (0, 1))
    if heads > 1:
        enter(1, (2, 3))
    send_halo(0)

    def step(n, _):
        @pl.when(n + 1 < heads)
        def _():
            send_halo(n + 1)

        entered(n, (2, 3))

        @pl.when(n + 3 < heads)
        def _():
            enter(n + 3, (0, 1))

        @pl.when(n + 2 < heads)
        def _():
            enter(n + 2, (2, 3))

        @pl.when(has_before)
        def _():
            halo(n, 0).wait_recv()
            halo(n, 1).wait_recv()

        def after_tile(at):
            @pl.when(has_before)
            def _():
                rows = pl.ds(pl.multiple_of(at * TILE, TILE), TILE)
                dk_far[n, rows, :] = (dk[n, rows, :] * query_scale).astype(jnp.bfloat16)
                dv_far[n, rows, :] = dv[n, rows, :].astype(jnp.bfloat16)
                back(n, 0, at).start()
                back(n, 1, at).start()

            for m in range(TILE // length):
                d = lax.rem(at * (TILE // length) + m - me + members, members)

                @pl.when(d == 0)
                def _():
                    exit_own(n, 0).start()
                    exit_own(n, 1).start()

                @pl.when(d > 0)
                def _():
                    exit_copy(n, d, 0).start()
                    exit_copy(n, d, 1).start()

        attend(
            n, factor, jnp.logical_not(has_before), qb, gb, kb, vb, kt, vt, probs_b, dscores_b, ob, dqb, dk, dv, after_tile
        )

        @pl.when(n > 0)
        def _():
            finish(n - 1)

        return 0

    lax.fori_loop(0, heads, step, 0)
    finish(heads - 1)

    def drain(n, _):
        for a in range(4):
            exit_own(n, a).wait()
            for d in range(1, members):
                entry(n, d, a).wait_send()
                exit_copy(n, d, a).wait()

        @pl.when(has_after)
        def _():
            halo(n, 0).wait_send()
            halo(n, 1).wait_send()

        @pl.when(has_before)
        def _():
            for c in range(chunks):
                back(n, 0, c).wait_send()
                back(n, 1, c).wait_send()

        return 0

    lax.fori_loop(0, heads, drain, 0)


def body(queries, keys, values, output_cotangent):
    length = queries.shape[0]
    side = lax.axis_size("head")
    near = WINDOW_TOKENS // (length * side)
    members = near * side
    width = HEAD_SIZE
    heads = keys.shape[1] // width // members
    factor = queries.shape[1] // keys.shape[1]
    wide = factor * width
    low, high = jnp.bfloat16, jnp.float32
    window = WINDOW_TOKENS
    pairs = heads * 2 * window * TILE * 6 * factor * width
    results = pl.pallas_call(
        functools.partial(kernel, near, heads, factor),
        out_shape=[jax.ShapeDtypeStruct(x.shape, x.dtype) for x in (queries, queries, keys, values)],
        in_specs=[pl.BlockSpec(memory_space=pl.ANY)] * 4,
        out_specs=[pl.BlockSpec(memory_space=pl.ANY)] * 4,
        scratch_shapes=[
            pltpu.VMEM((heads, window, wide), low),
            pltpu.VMEM((heads, window, wide), low),
            pltpu.VMEM((heads, 2 * window, width), low),
            pltpu.VMEM((heads, 2 * window, width), low),
            pltpu.VMEM((width, 2 * window), low),
            pltpu.VMEM((width, 2 * window), low),
            pltpu.VMEM((1, window + TILE, factor * TILE), low),
            pltpu.VMEM((1, window + TILE, factor * TILE), low),
            pltpu.VMEM((heads, window, wide), low),
            pltpu.VMEM((heads, window, wide), low),
            pltpu.VMEM((heads, 2 * window, width), high),
            pltpu.VMEM((heads, 2 * window, width), high),
            *[pltpu.VMEM((heads, window, width), low)] * 6,
            pltpu.SemaphoreType.DMA((heads, members, 4)),
            pltpu.SemaphoreType.DMA((heads, members, 4)),
            *[pltpu.SemaphoreType.DMA((heads, 2))] * 2,
            *[pltpu.SemaphoreType.DMA((heads, 2, window // TILE))] * 2,
            pltpu.SemaphoreType.DMA((heads, members, 4)),
            pltpu.SemaphoreType.DMA((heads, members, 4)),
        ],
        compiler_params=pltpu.CompilerParams(
            collective_id=0, has_side_effects=True, vmem_limit_bytes=40 * 1024 * 1024
        ),
        cost_estimate=pl.CostEstimate(flops=pairs * 2, bytes_accessed=24 * queries.size, transcendentals=0),
    )(queries, keys, values, output_cotangent)
    return tuple(results)


def solution(mesh):
    spec = P(("seq", "head"), None)
    return jax.shard_map(
        body,
        mesh=mesh,
        in_specs=(spec,) * 4,
        out_specs=(spec,) * 4,
        check_vma=False,
    )
```

```python
import functools

import jax
import jax.numpy as jnp
from jax import lax
from jax.experimental import pallas as pl
from jax.experimental.pallas import tpu as pltpu
from jax.sharding import PartitionSpec as P

HEAD_SIZE = 128
WINDOW_TOKENS = 1024
TILE = 256
MESH = pl.DeviceIdType.MESH

query_scale = 168.0 ** (-0.5)
exponent_scale = query_scale * 1.4426950408889634
HIDDEN = -1e30


def matmul(left, right):
    return jnp.dot(left, right, preferred_element_type=jnp.float32)


def turned(value):
    return value.astype(jnp.float32).T


def attend(n, factor, first, qb, gb, kb, vb, kt, vt, probs_b, dscores_b, ob, dqb, dk, dv, after_tile):
    width = HEAD_SIZE
    chunks = WINDOW_TOKENS // TILE
    span = WINDOW_TOKENS + TILE
    dk[n] = jnp.zeros(dk.shape[1:], jnp.float32)
    dv[n] = jnp.zeros(dv.shape[1:], jnp.float32)

    def turn(at, _):
        row = pl.multiple_of(at * TILE, TILE)
        kt[:, pl.ds(row, TILE)] = turned(kb[n, pl.ds(row, TILE), :]).astype(jnp.bfloat16)
        vt[:, pl.ds(row, TILE)] = turned(vb[n, pl.ds(row, TILE), :]).astype(jnp.bfloat16)
        return 0

    lax.fori_loop(0, kb.shape[1] // TILE, turn, 0)
    across = factor * TILE
    key_at = lax.broadcasted_iota(jnp.int32, (TILE, across), 0)
    query_at = lax.broadcasted_iota(jnp.int32, (TILE, across), 1) % TILE

    def block(at, spot):
        row = pl.multiple_of(at * TILE, TILE)
        slab = pl.ds(row, span)
        rows = [pl.ds(pl.multiple_of(row + c * TILE, TILE), TILE) for c in range(chunks + 1)]
        here = [slice(c * TILE, (c + 1) * TILE) for c in range(chunks + 1)]
        shift = [
            jnp.where(jnp.logical_and(first, at + c < chunks), -HIDDEN, 0.0) for c in range(chunks)
        ] + [0.0]
        q = jnp.concatenate([qb[n, pl.ds(row, TILE), r * width : (r + 1) * width] for r in range(factor)], 0)
        g = jnp.concatenate([gb[n, pl.ds(row, TILE), r * width : (r + 1) * width] for r in range(factor)], 0)
        g_turned = turned(g)
        q_t, g_t = turned(q).astype(jnp.bfloat16), g_turned.astype(jnp.bfloat16)
        scores = []
        top = None
        for c in range(chunks + 1):
            s = matmul(kb[n, rows[c], :], q_t)
            if c == 0:
                s = jnp.where(key_at > query_at, s, HIDDEN)
            if c == chunks:
                s = jnp.where(key_at <= query_at, s, HIDDEN)
            scores.append(s)
            most = jnp.max(s, axis=0, keepdims=True) - shift[c]
            top = most if top is None else jnp.maximum(top, most)
        total = None
        powers, dprobs = [], []
        for c in range(chunks + 1):
            dprobs.append(matmul(vb[n, rows[c], :], g_t))
            e = jnp.exp2(scores[c] * exponent_scale - (top + shift[c]) * exponent_scale)
            part = jnp.sum(e, axis=0, keepdims=True)
            total = part if total is None else total + part
            powers.append(e)
        inverse = 1.0 / total
        probs = []
        for c in range(chunks + 1):
            probs.append(powers[c] * inverse)
            probs_b[spot, here[c], :] = probs[c].astype(jnp.bfloat16)
        out = matmul(vt[:, slab], probs_b[spot])
        out_b = out.astype(jnp.bfloat16).astype(jnp.float32)
        delta = jnp.sum(g_turned * out_b, axis=0, keepdims=True)
        for r in range(factor):
            ob[n, pl.ds(row, TILE), r * width : (r + 1) * width] = out[:, r * TILE : (r + 1) * TILE].T.astype(jnp.bfloat16)
        for c in range(chunks + 1):
            dscores_b[spot, here[c], :] = (probs[c] * (dprobs[c] - delta)).astype(jnp.bfloat16)
            dv[n, rows[c], :] += matmul(probs_b[spot, here[c], :], g)
        dq = matmul(kt[:, slab], dscores_b[spot]) * query_scale
        for c in range(chunks + 1):
            dk[n, rows[c], :] += matmul(dscores_b[spot, here[c], :], q)
        for r in range(factor):
            dqb[n, pl.ds(row, TILE), r * width : (r + 1) * width] = dq[:, r * TILE : (r + 1) * TILE].T.astype(jnp.bfloat16)

    def pair(at, _):
        block(2 * at, 0)
        block(2 * at + 1, 1)
        after_tile(2 * at)
        after_tile(2 * at + 1)
        return 0

    lax.fori_loop(0, WINDOW_TOKENS // TILE // 2, pair, 0)


def kernel(
    near, heads, factor, queries, keys, values, cotangent, attended, grad_queries, key_gradient, value_gradient,
    qb, gb, kb, vb, kt, vt, probs_b, dscores_b, ob, dqb, dk, dv, dk_far, dv_far, dk_back, dv_back, dk_own, dv_own,
    in_send, in_recv, halo_send, halo_recv, back_send, back_recv, out_send, out_recv,
):
    length = queries.shape[0]
    width = HEAD_SIZE
    side = lax.axis_size("head")
    members = near * side
    teams = lax.axis_size("seq") // near
    seq, head = lax.axis_index("seq"), lax.axis_index("head")
    team = seq // near
    me = lax.rem(seq, near) * side + head
    has_before, has_after = team > 0, team < teams - 1

    def device(team_at, member):
        return (team_at * near + member // side, lax.rem(member, side))

    ahead, behind = device(team + 1, me), device(team - 1, me)
    barrier = pltpu.get_barrier_semaphore()
    for d in range(1, members):
        pl.semaphore_signal(barrier, inc=1, device_id=device(team, lax.rem(me + d, members)), device_id_type=MESH)

    @pl.when(has_after)
    def _():
        pl.semaphore_signal(barrier, inc=1, device_id=ahead, device_id_type=MESH)

    @pl.when(has_before)
    def _():
        pl.semaphore_signal(barrier, inc=1, device_id=behind, device_id_type=MESH)

    pl.semaphore_wait(barrier, members - 1 + has_after.astype(jnp.int32) + has_before.astype(jnp.int32))

    def columns(member, n, size):
        return pl.ds(pl.multiple_of((member * heads + n) * size, size), size)

    def token_rows(member, start=0):
        return pl.ds(pl.multiple_of(start + member * length, length), length)

    wide = factor * width
    entering = ((keys, width, kb, WINDOW_TOKENS), (values, width, vb, WINDOW_TOKENS), (queries, wide, qb, 0), (cotangent, wide, gb, 0))
    leaving = ((ob, wide, attended), (dqb, wide, grad_queries), (dk_own, width, key_gradient), (dv_own, width, value_gradient))

    def entry(n, d, a):
        source, size, buffer, start = entering[a]
        other = lax.rem(me + d, members)
        src = source.at[:, columns(other, n, size)]
        dst = buffer.at[n, token_rows(me, start), :]
        if d == 0:
            return pltpu.make_async_copy(src, dst, in_recv.at[n, 0, a])
        return pltpu.make_async_remote_copy(
            src, dst, in_send.at[n, d, a], in_recv.at[n, d, a], device_id=device(team, other), device_id_type=MESH
        )

    def enter(n, which):
        for a in which:
            for d in (*range(1, members), 0):
                entry(n, d, a).start()

    def entered(n, which):
        for a in which:
            entry(n, 0, a).wait()
            for d in range(1, members):
                entry(n, d, a).wait_recv()

    def halo(n, a):
        buffer = entering[a][2]
        return pltpu.make_async_remote_copy(
            buffer.at[n, pl.ds(WINDOW_TOKENS, WINDOW_TOKENS), :], buffer.at[n, pl.ds(0, WINDOW_TOKENS), :],
            halo_send.at[n, a], halo_recv.at[n, a], device_id=ahead, device_id_type=MESH,
        )

    chunks = WINDOW_TOKENS // TILE

    def back(n, a, c):
        source, target = ((dk_far, dk_back), (dv_far, dv_back))[a]
        rows = pl.ds(pl.multiple_of(c * TILE, TILE), TILE)
        return pltpu.make_async_remote_copy(
            source.at[n, rows, :], target.at[n, rows, :], back_send.at[n, a, c], back_recv.at[n, a, c],
            device_id=behind, device_id_type=MESH,
        )

    def exit_own(n, a):
        buffer, size, target = leaving[a]
        return pltpu.make_async_copy(
            buffer.at[n, token_rows(me), :], target.at[:, columns(me, n, size)], out_recv.at[n, 0, a]
        )

    def exit_copy(n, d, a):
        buffer, size, target = leaving[a]
        other = lax.rem(me + d, members)
        return pltpu.make_async_remote_copy(
            buffer.at[n, token_rows(other), :], target.at[:, columns(me, n, size)],
            out_send.at[n, d, a], out_recv.at[n, d, a], device_id=device(team, other), device_id_type=MESH,
        )

    def leave(n, which):
        for a in which:
            for d in range(1, members):
                exit_copy(n, d, a).start()
            exit_own(n, a).start()

    def send_halo(n):
        entered(n, (0, 1))

        @pl.when(has_after)
        def _():
            halo(n, 0).start()
            halo(n, 1).start()

    def finish(n):
        for a, (total, received, result, factor_of) in enumerate(
            ((dk, dk_back, dk_own, query_scale), (dv, dv_back, dv_own, 1.0))
        ):
            own = total[n, pl.ds(WINDOW_TOKENS, WINDOW_TOKENS), :] * factor_of

            @pl.when(has_after)
            def _():
                for c in range(chunks):
                    back(n, a, c).wait_recv()
                result[n] = (own + received[n].astype(jnp.float32)).astype(jnp.bfloat16)

            @pl.when(jnp.logical_not(has_after))
            def _():
                result[n] = own.astype(jnp.bfloat16)

        leave(n, (2, 3))

    @pl.when(jnp.logical_not(has_before))
    def _():
        for n in range(heads):
            kb[n, pl.ds(0, WINDOW_TOKENS), :] = jnp.zeros((WINDOW_TOKENS, width), kb.dtype)
            vb[n, pl.ds(0, WINDOW_TOKENS), :] = jnp.zeros((WINDOW_TOKENS, width), vb.dtype)

    enter(0, (0, 1))
    if heads > 1:
        enter(1, (0, 1))
    enter(0, (2, 3))
    if heads > 2:
        enter(2, (0, 1))
    if heads > 1:
        enter(1, (2, 3))
    send_halo(0)

    def step(n, _):
        @pl.when(n + 1 < heads)
        def _():
            send_halo(n + 1)

        entered(n, (2, 3))

        @pl.when(n + 3 < heads)
        def _():
            enter(n + 3, (0, 1))

        @pl.when(n + 2 < heads)
        def _():
            enter(n + 2, (2, 3))

        @pl.when(has_before)
        def _():
            halo(n, 0).wait_recv()
            halo(n, 1).wait_recv()

        def after_tile(at):
            @pl.when(has_before)
            def _():
                rows = pl.ds(pl.multiple_of(at * TILE, TILE), TILE)
                dk_far[n, rows, :] = (dk[n, rows, :] * query_scale).astype(jnp.bfloat16)
                dv_far[n, rows, :] = dv[n, rows, :].astype(jnp.bfloat16)
                back(n, 0, at).start()
                back(n, 1, at).start()

            for m in range(TILE // length):
                d = lax.rem(at * (TILE // length) + m - me + members, members)

                @pl.when(d == 0)
                def _():
                    exit_own(n, 0).start()
                    exit_own(n, 1).start()

                @pl.when(d > 0)
                def _():
                    exit_copy(n, d, 0).start()
                    exit_copy(n, d, 1).start()

        attend(
            n, factor, jnp.logical_not(has_before), qb, gb, kb, vb, kt, vt, probs_b, dscores_b, ob, dqb, dk, dv, after_tile
        )

        @pl.when(n > 0)
        def _():
            finish(n - 1)

        return 0

    lax.fori_loop(0, heads, step, 0)
    finish(heads - 1)

    def drain(n, _):
        for a in range(4):
            exit_own(n, a).wait()
            for d in range(1, members):
                entry(n, d, a).wait_send()
                exit_copy(n, d, a).wait()

        @pl.when(has_after)
        def _():
            halo(n, 0).wait_send()
            halo(n, 1).wait_send()

        @pl.when(has_before)
        def _():
            for c in range(chunks):
                back(n, 0, c).wait_send()
                back(n, 1, c).wait_send()

        return 0

    lax.fori_loop(0, heads, drain, 0)


def hand_over(*refs):
    for source, target in zip(refs[:4], refs[4:]):
        target[...] = source[...]


def body(queries, keys, values, output_cotangent):
    length = queries.shape[0]
    side = lax.axis_size("head")
    near = WINDOW_TOKENS // (length * side)
    members = near * side
    width = HEAD_SIZE
    heads = keys.shape[1] // width // members
    factor = queries.shape[1] // keys.shape[1]
    wide = factor * width
    low, high = jnp.bfloat16, jnp.float32
    window = WINDOW_TOKENS
    pairs = heads * 2 * window * TILE * 6 * factor * width
    results = pl.pallas_call(
        functools.partial(kernel, near, heads, factor),
        out_shape=[jax.ShapeDtypeStruct(x.shape, x.dtype) for x in (queries, queries, keys, values)],
        in_specs=[pl.BlockSpec(memory_space=pl.ANY)] * 4,
        out_specs=[pl.BlockSpec(memory_space=pl.ANY)] * 4,
        scratch_shapes=[
            pltpu.VMEM((heads, window, wide), low),
            pltpu.VMEM((heads, window, wide), low),
            pltpu.VMEM((heads, 2 * window, width), low),
            pltpu.VMEM((heads, 2 * window, width), low),
            pltpu.VMEM((width, 2 * window), low),
            pltpu.VMEM((width, 2 * window), low),
            pltpu.VMEM((2, window + TILE, factor * TILE), low),
            pltpu.VMEM((2, window + TILE, factor * TILE), low),
            pltpu.VMEM((heads, window, wide), low),
            pltpu.VMEM((heads, window, wide), low),
            pltpu.VMEM((heads, 2 * window, width), high),
            pltpu.VMEM((heads, 2 * window, width), high),
            *[pltpu.VMEM((heads, window, width), low)] * 6,
            pltpu.SemaphoreType.DMA((heads, members, 4)),
            pltpu.SemaphoreType.DMA((heads, members, 4)),
            *[pltpu.SemaphoreType.DMA((heads, 2))] * 2,
            *[pltpu.SemaphoreType.DMA((heads, 2, window // TILE))] * 2,
            pltpu.SemaphoreType.DMA((heads, members, 4)),
            pltpu.SemaphoreType.DMA((heads, members, 4)),
        ],
        compiler_params=pltpu.CompilerParams(
            collective_id=0, has_side_effects=True, vmem_limit_bytes=60 * 1024 * 1024
        ),
        cost_estimate=pl.CostEstimate(flops=pairs * 2, bytes_accessed=24 * queries.size, transcendentals=0),
    )(queries, keys, values, output_cotangent)
    return tuple(
        pl.pallas_call(
            hand_over,
            grid=(4,),
            out_shape=[jax.ShapeDtypeStruct(x.shape, x.dtype) for x in results],
            in_specs=[pl.BlockSpec((x.shape[0] // 4, x.shape[1]), lambda i: (i, 0)) for x in results],
            out_specs=[pl.BlockSpec((x.shape[0] // 4, x.shape[1]), lambda i: (i, 0)) for x in results],
            compiler_params=pltpu.CompilerParams(vmem_limit_bytes=60 * 1024 * 1024),
        )(*results)
    )


def solution(mesh):
    spec = P(("seq", "head"), None)
    return jax.shard_map(
        body,
        mesh=mesh,
        in_specs=(spec,) * 4,
        out_specs=(spec,) * 4,
        check_vma=False,
    )
```
